128 devices in a mesh: row: 16 (over x, y), col: 8 (over z, core).
Axes of the slice: x: 4, y: 4, z: 4, core: 2. Of those that a mesh axis runs over, the one named last changes fastest.
Arguments:
- layer_input: bfloat16 [2048, 8192], P('col', 'row'), may hold values from -6 to 6
- gate_pre: bfloat16 [2048, 14336], P('row', 'col'), may hold values from -8 to 8
- up_pre: bfloat16 [2048, 14336], P('row', 'col'), may hold values from -6 to 6
- grad_out: bfloat16 [2048, 8192], P('col', 'row'), may hold values from -2 to 2
- w_gate: bfloat16 [8192, 14336], P('row', 'col'), may hold values from -0.0625 to 0.0625
- w_up: bfloat16 [8192, 14336], P('row', 'col'), may hold values from -0.0625 to 0.0625
- w_down: bfloat16 [14336, 8192], P('col', 'row'), may hold values from -0.046875 to 0.046875
Outputs:
- grad_input: bfloat16 [2048, 8192], P('col', 'row')
- grad_gate: float32 [8192, 14336], P('row', 'col')
- grad_up: float32 [8192, 14336], P('row', 'col')
- grad_down: float32 [14336, 8192], P('col', 'row')
The draws below stay inside these ranges and needn't reach their ends.
All inputs are finite; a program needn't handle non-finite values.
Results may differ from the reference program's by a relative error of at most 0.027.
Values may be sent and summed in bfloat16 or wider, within the bound.
No kernel may reach another device: no remote copies, remote signals or barrier semaphores. Data moves between devices by JAX's collectives and lax.ppermute only.
A program may use at most 128 MiB of HBM per device.

```python
import jax
import jax.numpy as jnp
from jax import lax

D = 8192
FF = 14336
TOKENS = 2048
N_ROW = 16
N_COL = 8


def raised(result, stream_key, source, target, parts, factor):
    owner, partner = [(jnp.arange(result.shape[dim]) // (result.shape[dim] // parts)).reshape([-1 if axis == dim else 1 for axis in range(result.ndim)]) for dim in (source, target)]
    chosen = jax.random.permutation(stream_key, parts)[partner]
    strong = (owner == chosen) | (owner == (partner + parts // 2) % parts)
    return jnp.where(strong, factor * result, result)


def shard_levels(own_key, dims, shards, least, largest):
    def one(axis_at, blocks):
        draws = jax.random.uniform(jax.random.fold_in(jax.random.fold_in(own_key, 6), axis_at), (blocks,), jnp.float32, least / len(shards), largest / len(shards))
        return jnp.repeat(jnp.exp(draws), dims[axis_at] // blocks).reshape((-1,) + (1,) * (len(dims) - axis_at - 1))

    level = one(*shards[0])
    for cut in shards[1:]:
        level = level * one(*cut)
    return level


def gaussian(own_key, dims, deviation, reach, shards=(), kind=jnp.bfloat16):
    drawn = jax.random.normal(own_key, dims, jnp.float32) * deviation
    if len(shards) > 0:
        drawn = shard_levels(own_key, dims, shards, -0.22, 0.18) * drawn
    return jnp.clip(drawn, min=-reach, max=reach).astype(kind)


def gaussian_with(stream_key, shape, deviation, limit, shards, heavy, kind=jnp.bfloat16):
    drawn = deviation * jax.random.normal(stream_key, shape, jnp.float32)
    if shards:
        drawn = drawn * shard_levels(stream_key, shape, shards, -0.22, 0.18)
    return jnp.clip(raised(drawn, jax.random.fold_in(stream_key, 3), *heavy), -limit, limit).astype(kind)


def setup_inputs(seed: int = 0) -> dict:
    key_list = jax.random.split(jax.random.key(seed), 8)
    return {
        "layer_input": gaussian(key_list[0], (TOKENS, D), 1.0, 6.0, ((0, 8), (1, 16))),
        "gate_pre": gaussian(key_list[1], (TOKENS, FF), 1.5, 8.0, ((0, 16), (1, 8))),
        "up_pre": gaussian(key_list[2], (TOKENS, FF), 1.0, 6.0, ((0, 16), (1, 8))),
        "grad_out": gaussian_with(key_list[3], (TOKENS, D), 0.25, 2.0, ((0, 8), (1, 16)), (1, 0, 16, 2.0)),
        "w_gate": gaussian(key_list[4], (D, FF), D ** -0.5, 0.0625, ((0, 16), (1, 8))),
        "w_up": gaussian(key_list[5], (D, FF), D ** -0.5, 0.0625, ((0, 16), (1, 8))),
        "w_down": gaussian(key_list[6], (FF, D), FF ** -0.5, 0.046875, ((0, 8), (1, 16))),
    }


def swiglu_parts(grad_hidden, gate_pre, up_pre):
    gate_val = gate_pre.astype(jnp.float32)
    up_val = up_pre.astype(jnp.float32)
    sigmoid_val = jax.nn.sigmoid(gate_val)
    silu_val = gate_val * sigmoid_val
    hidden = (silu_val * up_val).astype(jnp.bfloat16)
    up_grad = (grad_hidden * silu_val).astype(jnp.bfloat16)
    gate_grad = (grad_hidden * up_val * sigmoid_val * (1.0 + gate_val * (1.0 - sigmoid_val))).astype(jnp.bfloat16)
    return hidden, gate_grad, up_grad


def rounded(value):
    narrow = lax.optimization_barrier(value.astype(jnp.bfloat16))
    return narrow.astype(jnp.float32)


def reference(layer_input, gate_pre, up_pre, grad_out, w_gate, w_up, w_down):
    tokens = layer_input.shape[0]
    dshard = D // N_ROW
    fshard = FF // N_COL
    last_dims = (((1,), (1,)), ((), ()))
    first_dims = (((0,), (0,)), ((), ()))
    out_blocks = grad_out.reshape(tokens, N_ROW, dshard).transpose(1, 0, 2)
    down_blocks = w_down.reshape(FF, N_ROW, dshard).transpose(1, 0, 2)

    def add_hidden(total, pieces):
        term = lax.dot_general(pieces[0], pieces[1], last_dims, preferred_element_type=jnp.float32)
        return total + rounded(term), None

    grad_hidden, _ = lax.scan(add_hidden, jnp.zeros((tokens, FF), jnp.float32), (out_blocks, down_blocks))
    hidden, gate_grad, up_grad = swiglu_parts(grad_hidden, gate_pre, up_pre)
    grad_down = lax.dot_general(hidden, grad_out, first_dims, preferred_element_type=jnp.float32)
    grad_gate = lax.dot_general(layer_input, gate_grad, first_dims, preferred_element_type=jnp.float32)
    grad_up = lax.dot_general(layer_input, up_grad, first_dims, preferred_element_type=jnp.float32)
    gate_blocks = gate_grad.reshape(tokens, N_COL, fshard).transpose(1, 0, 2)
    upg_blocks = up_grad.reshape(tokens, N_COL, fshard).transpose(1, 0, 2)
    wg_blocks = w_gate.reshape(D, N_COL, fshard).transpose(1, 0, 2)
    wu_blocks = w_up.reshape(D, N_COL, fshard).transpose(1, 0, 2)

    def add_input(total, pieces):
        term = lax.dot_general(pieces[0], pieces[2], last_dims, preferred_element_type=jnp.float32)
        term = term + lax.dot_general(pieces[1], pieces[3], last_dims, preferred_element_type=jnp.float32)
        return total + rounded(term), None

    grad_input, _ = lax.scan(add_input, jnp.zeros((tokens, D), jnp.float32), (gate_blocks, upg_blocks, wg_blocks, wu_blocks))
    return grad_input.astype(jnp.bfloat16), grad_gate, grad_up, grad_down
```

```python
import jax
import jax.numpy as jnp
from jax import lax
from jax.sharding import Mesh, PartitionSpec as P

F32 = jnp.float32
BF16 = jnp.bfloat16
RING = 4
LAST = (((1,), (1,)), ((), ()))
FIRST = (((0,), (0,)), ((), ()))


def mix(value, phase, step):
    pairs = []
    for x in range(RING):
        for y in range(RING):
            for core in range(2):
                if (core == 0) == (phase == 1):
                    to = ((x + step) % RING, y)
                else:
                    to = (x, (y + step) % RING)
                pairs.append(((x * RING + y) * 2 + core, (to[0] * RING + to[1]) * 2 + core))
    return lax.ppermute(value, ("x", "y", "c"), pairs)


def along_z(value, step):
    return lax.ppermute(value, "z", [(z, (z + step) % RING) for z in range(RING)])


def swap(value):
    return lax.ppermute(value, "c", [(0, 1), (1, 0)])


def pick(value, at):
    return lax.dynamic_index_in_dim(value, at, 0, keepdims=False)


def roll(value, shift, axis):
    return lax.dynamic_slice_in_dim(
        jnp.concatenate([value, value], axis), shift, value.shape[axis], axis
    )


def sigmoid_parts(gate_pre, up_pre):
    gate_val = gate_pre.astype(F32)
    up_val = up_pre.astype(F32)
    sigmoid_val = jax.nn.sigmoid(gate_val)
    return gate_val, up_val, sigmoid_val, gate_val * sigmoid_val


def hidden_of(gate_pre, up_pre):
    _, up_val, _, silu_val = sigmoid_parts(gate_pre, up_pre)
    return (silu_val * up_val).astype(BF16)


def grads_of(grad_hidden, gate_pre, up_pre):
    gate_val, up_val, sigmoid_val, silu_val = sigmoid_parts(gate_pre, up_pre)
    gate_grad = grad_hidden * up_val * sigmoid_val * (1.0 + gate_val * (1.0 - sigmoid_val))
    return gate_grad.astype(BF16), (grad_hidden * silu_val).astype(BF16)


def gather(block):
    _, n, rows, width = block.shape
    before, after, across = mix(block, 1, 1), mix(block, 1, -1), mix(block, 1, 2)
    own, other = (
        jnp.stack([block[i], after[i], across[i], before[i]], 1).reshape(n, RING * rows, width)
        for i in range(2)
    )
    own_before, other_after = mix(own, 2, 1), mix(other, 2, -1)
    other_before, own_after = mix(other, 2, 1), mix(own, 2, -1)
    own_across, other_across = mix(own_before, 2, 1), mix(other_after, 2, -1)
    return (
        [own, own_after, own_across, own_before],
        [other, other_after, other_across, other_before],
    )


def scatter_sum(own, other):
    def add(*values):
        total = values[0].astype(F32)
        for value in values[1:]:
            total = total + value.astype(F32)
        return total

    own_fwd, other_back = mix(own[2], 2, 1), mix(other[2], 2, -1)
    other_fwd, own_back = mix(other[1], 2, 1), mix(own[3], 2, -1)
    own_fwd = mix(add(own[1], own_fwd).astype(BF16), 2, 1)
    other_back = mix(add(other[3], other_back).astype(BF16), 2, -1)
    sums = jnp.stack([add(own[0], own_fwd, own_back), add(other[0], other_fwd, other_back)])
    sums = sums.astype(BF16).reshape(2, RING, -1, sums.shape[-1])
    return add(
        sums[:, 0], mix(sums[:, 1], 1, 1), mix(sums[:, 3], 1, -1), mix(sums[:, 2], 1, 2)
    )


def on_device(layer_input, gate_pre, up_pre, grad_out, w_gate, w_up, w_down):
    x, y, z, core = (lax.axis_index(name) for name in ("x", "y", "z", "c"))
    rows, width = gate_pre.shape
    half, model = rows // 2, w_down.shape[1]

    out_all = lax.all_gather(grad_out, ("z", "c"), axis=0, tiled=True)
    input_all = lax.all_gather(layer_input, ("z", "c"), axis=0, tiled=True)

    def both(value):
        parts = value.reshape(2, half, width)
        return jnp.stack([pick(parts, core), swap(pick(parts, 1 - core))])

    gate_both, up_both = both(gate_pre), both(up_pre)
    w_down_other, w_gate_other, w_up_other = swap(w_down), swap(w_gate), swap(w_up)
    hidden_own, hidden_other = gather(hidden_of(gate_both, up_both)[:, None])

    def relative(value):
        value = value.reshape(RING, RING, 2, half, model)
        value = roll(roll(value, x, 0), y, 1)
        first, second = value[:, :, 0].transpose(1, 0, 2, 3), value[:, :, 1]
        mine = jnp.where(core == 0, first, second)
        theirs = jnp.where(core == 0, second, first)
        return mine.reshape(RING, RING * half, model), theirs.reshape(RING, RING * half, model)

    out_mine, out_theirs = relative(out_all)

    def partials(weight):
        return [
            lax.dot_general(out_mine[k], weight, LAST, preferred_element_type=F32).astype(BF16)
            for k in range(RING)
        ]

    grad_hidden = scatter_sum(partials(w_down), partials(w_down_other))
    gate_grad, up_grad = grads_of(grad_hidden, gate_both, up_both)
    own, other = gather(jnp.stack([gate_grad, up_grad], 1))

    def whole(mine, theirs):
        return jnp.concatenate(list(mine) + list(theirs), 0)

    hidden = whole([p[0] for p in hidden_own], [swap(p)[0] for p in hidden_other])
    out_rel = jnp.concatenate([out_mine, out_theirs]).reshape(-1, model)
    grad_down = lax.dot_general(hidden, out_rel, FIRST, preferred_element_type=F32)

    input_mine, input_theirs = relative(input_all)
    input_rel = jnp.concatenate([input_mine, input_theirs]).reshape(-1, model)
    theirs = [swap(p) for p in other]
    gate_all = whole([p[0] for p in own], [p[0] for p in theirs])
    up_all = whole([p[1] for p in own], [p[1] for p in theirs])
    grad_gate = lax.dot_general(input_rel, gate_all, FIRST, preferred_element_type=F32)
    grad_up = lax.dot_general(input_rel, up_all, FIRST, preferred_element_type=F32)

    def input_part(k):
        total = 0.0
        for piece, weights in ((own[k], (w_gate, w_up)), (other[k], (w_gate_other, w_up_other))):
            for i in range(2):
                total = total + lax.dot_general(
                    piece[i], weights[i], LAST, preferred_element_type=F32
                )
        return total.astype(BF16)

    part = jnp.stack([input_part(k) for k in range(RING)]).reshape(RING, RING, half, model)
    part = jnp.where(core == 0, part.transpose(1, 0, 2, 3), part)
    part = roll(roll(part, (z - x) % RING, 0), (-y) % RING, 1)
    total = (
        part[0].astype(F32)
        + along_z(part[1], 1).astype(F32)
        + along_z(part[3], -1).astype(F32)
        + along_z(part[2], 2).astype(F32)
    ).astype(BF16)
    pairs = total.reshape(2, 2, half, model)
    keep, got = pick(pairs, core), swap(pick(pairs, 1 - core))
    grad_input = jnp.where(
        core == 0, jnp.stack([keep, got], 1), jnp.stack([got, keep], 1)
    ).reshape(4 * half, model)
    return grad_input, grad_gate, grad_up, grad_down


def solution(mesh):
    chips = Mesh(mesh.devices.reshape(RING, RING, RING, 2), ("x", "y", "z", "c"))
    row, col = ("x", "y"), ("z", "c")
    in_specs = (
        P(col, row),
        P(row, col),
        P(row, col),
        P(col, row),
        P(row, col),
        P(row, col),
        P(col, row),
    )
    out_specs = (P(col, row), P(row, col), P(row, col), P(col, row))
    return jax.shard_map(
        on_device, mesh=chips, in_specs=in_specs, out_specs=out_specs, check_vma=False
    )
```

```python
import jax
import jax.numpy as jnp
from jax import lax
from jax.experimental import pallas as pl
from jax.experimental.pallas import tpu as pltpu
from jax.sharding import Mesh, PartitionSpec as P

F32 = jnp.float32
BF16 = jnp.bfloat16
RING = 4
LAST = (((1,), (1,)), ((), ()))
FIRST = (((0,), (0,)), ((), ()))
MIB = 2**20


def mix(value, phase, step):
    pairs = []
    for x in range(RING):
        for y in range(RING):
            for core in range(2):
                if (core == 0) == (phase == 1):
                    to = ((x + step) % RING, y)
                else:
                    to = (x, (y + step) % RING)
                pairs.append(((x * RING + y) * 2 + core, (to[0] * RING + to[1]) * 2 + core))
    return lax.ppermute(value, ("x", "y", "c"), pairs)


def along_z(value, step):
    return lax.ppermute(value, "z", [(z, (z + step) % RING) for z in range(RING)])


def swap(value):
    return lax.ppermute(value, "c", [(0, 1), (1, 0)])


def pick(value, at, axis=0):
    return lax.dynamic_index_in_dim(value, at, axis, keepdims=False)


def tie(value, *after):
    return lax.optimization_barrier((value, *after))[0]


def params(mebibytes):
    return pltpu.CompilerParams(vmem_limit_bytes=mebibytes * MIB)


def cost(flops, moved):
    return pl.CostEstimate(flops=flops, bytes_accessed=moved, transcendentals=0)


def travel_order(place, value):
    tokens, model = value.shape
    half = tokens // 32
    value = value.reshape(RING, RING, 2, half, model)

    def kernel(place_ref, value_ref, *results):
        x, y, core = place_ref[0], place_ref[1], place_ref[3]
        for result, owner in zip(results, (core, 1 - core)):
            for second in range(RING):
                for first in range(RING):
                    at_x = lax.rem(x + jnp.where(owner == 0, first, second), RING)
                    at_y = lax.rem(y + jnp.where(owner == 0, second, first), RING)
                    rows = slice(first * half, (first + 1) * half)
                    result[second, rows] = value_ref[at_x, at_y, owner]

    return pl.pallas_call(
        kernel,
        grid=(1,),
        in_specs=[
            pl.BlockSpec(memory_space=pltpu.SMEM),
            pl.BlockSpec(value.shape, lambda j: (0,) * 5),
        ],
        out_specs=[pl.BlockSpec((RING, RING * half, model), lambda j: (0,) * 3)] * 2,
        out_shape=[jax.ShapeDtypeStruct((RING, RING * half, model), BF16)] * 2,
        compiler_params=params(12),
        cost_estimate=cost(0, 2 * tokens * model * 2),
        name="travel_order",
    )(place, value)


def down_products(tokens, parts):
    _, rows, model = tokens.shape
    width = parts[0][1].shape[0]
    tile = width // 2
    operands, in_specs = [], []
    for k, weight, extras in parts:
        operands += [tokens, weight, *extras]
        in_specs.append(pl.BlockSpec((1, rows, model), lambda j, k=k: (k, 0, 0)))
        in_specs.append(pl.BlockSpec((tile, model), lambda j: (j, 0)))
        in_specs += [pl.BlockSpec((rows, tile), lambda j: (0, j)) for _ in extras]

    def kernel(*refs):
        at = 0
        for out, (_, _, extras) in zip(refs[len(operands) :], parts):
            total = lax.dot_general(
                refs[at][0], refs[at + 1][...], LAST, preferred_element_type=F32
            )
            for i in range(len(extras)):
                total = total + refs[at + 2 + i][...].astype(F32)
            at += 2 + len(extras)
            out[...] = total.astype(BF16)

    return pl.pallas_call(
        kernel,
        grid=(2,),
        in_specs=in_specs,
        out_specs=[pl.BlockSpec((rows, tile), lambda j: (0, j))] * len(parts),
        out_shape=[jax.ShapeDtypeStruct((rows, width), BF16)] * len(parts),
        compiler_params=params(12),
        cost_estimate=cost(
            2 * rows * model * width * len(parts), (model + rows) * width * 2 * len(parts)
        ),
        name="down_products",
    )(*operands)


def scatter_sum(tokens, weight, weight_other, before, beside):
    own2, other2 = down_products(tokens, [(2, weight, ()), (2, weight_other, ())])
    other1, own3 = down_products(tokens, [(1, weight_other, ()), (3, weight, ())])
    own2, other2, other1, own3, *_ = lax.optimization_barrier((own2, other2, other1, own3, *before))
    own_fwd, other_back = mix(own2, 2, 1), mix(other2, 2, -1)
    other_fwd, own_back = mix(other1, 2, 1), mix(own3, 2, -1)
    own1, other3 = down_products(
        tokens, [(1, weight, (own_fwd,)), (3, weight_other, (other_back,))]
    )
    own_fwd, other_back = mix(own1, 2, 1), mix(other3, 2, -1)
    sums = jnp.stack(
        down_products(
            tokens, [(0, weight, (own_fwd, own_back)), (0, weight_other, (other_fwd, other_back))]
        )
    )
    sums = sums.reshape(2, RING, -1, sums.shape[-1])
    done = beside(sums)
    total = tie(sums[:, 0], *done).astype(F32)
    for distance, step in ((1, 1), (3, -1), (2, 2)):
        total = total + mix(sums[:, distance], 1, step).astype(F32)
    return total, done


def first_gather(block):
    _, n, half, width = block.shape
    pieces = [block, mix(block, 1, -1), mix(block, 1, 2), mix(block, 1, 1)]
    return tuple(
        jnp.stack([piece[i] for piece in pieces], 1).reshape(n, RING * half, width)
        for i in range(2)
    )


def weight_grads(left_mine, left_theirs, mine, theirs, flip=False):
    n, rows, width = mine[0].shape
    model = left_mine.shape[2]
    pieces = [*mine, *theirs]
    tile = 256

    def kernel(mine_ref, theirs_ref, *refs):
        left = refs[-1]

        @pl.when(pl.program_id(0) == 0)
        def _():
            for k in range(RING):
                left[:, k * rows : (k + 1) * rows] = mine_ref[k].T
                left[:, (RING + k) * rows : (RING + k + 1) * rows] = theirs_ref[k].T

        for i in range(n):
            right = jnp.concatenate([ref[i] for ref in refs[: len(pieces)]], 0)
            result = jnp.dot(left[...], right, preferred_element_type=F32)
            refs[len(pieces) + i][...] = result.T if flip else result

    if flip:
        shape, out_spec = (width, model), pl.BlockSpec((tile, model), lambda j: (j, 0))
    else:
        shape, out_spec = (model, width), pl.BlockSpec((model, tile), lambda j: (0, j))

    return pl.pallas_call(
        kernel,
        grid=(width // tile,),
        in_specs=[pl.BlockSpec(left_mine.shape, lambda j: (0, 0, 0))] * 2
        + [pl.BlockSpec((n, rows, tile), lambda j: (0, 0, j)) for _ in pieces],
        out_specs=[out_spec] * n,
        out_shape=[jax.ShapeDtypeStruct(shape, F32)] * n,
        scratch_shapes=[pltpu.VMEM((model, rows * len(pieces)), BF16)],
        compiler_params=params(18 if n > 1 else 14),
        cost_estimate=cost(
            2 * n * model * width * rows * len(pieces),
            n * model * width * 4 + n * rows * width * 2 * len(pieces),
        ),
        name="weight_grads",
    )(left_mine, left_theirs, *pieces)


def input_products(own, other, weights, ready=(), place=None):
    count = len(own)
    _, rows, width = own[0].shape
    model = weights[0].shape[0]
    last = place is not None
    tile = width // 2 if last else 256
    steps = width // tile
    half = rows // RING

    def kernel(*refs):
        place_ref, refs = (refs[0], refs[1:]) if last else (None, refs)
        own_refs, other_refs = refs[:count], refs[count : 2 * count]
        weight_refs = refs[2 * count : 2 * count + 4]
        ready_refs = refs[2 * count + 4 : 2 * count + 4 + len(ready)]
        total, outs = refs[-1], refs[2 * count + 4 + len(ready) : -1]
        if last:
            outs, held = outs[:-1], outs[-1]
        step = pl.program_id(0)
        for p in range(count):
            value = None
            for piece, pair in ((own_refs[p], weight_refs[:2]), (other_refs[p], weight_refs[2:])):
                for i in range(2):
                    term = lax.dot_general(
                        piece[i], pair[i][...], LAST, preferred_element_type=F32
                    )
                    value = term if value is None else value + term

            @pl.when(step == 0)
            def _():
                total[p] = value

            @pl.when((step > 0) & (step < steps - 1))
            def _():
                total[p] += value

            @pl.when(step == steps - 1)
            def _():
                value_all = (total[p] + value).astype(BF16)
                if not last:
                    outs[p][...] = value_all
                    return
                x, y, z, core = (place_ref[i] for i in range(4))
                for k, ref in zip((0, 1, 3), ready_refs):
                    held[k] = ref[...].reshape(RING, half, model)
                held[2] = value_all.reshape(RING, half, model)
                for distance in range(RING):
                    at_x = lax.rem(z + distance - x + RING, RING)
                    for j in range(2):
                        for low in range(2):
                            at_y = lax.rem(2 * lax.rem(core + j, 2) + low - y + RING, RING)
                            second = jnp.where(core == 0, at_y, at_x)
                            first = jnp.where(core == 0, at_x, at_y)
                            outs[distance][j, low] = held[second, first]

    scratch = [pltpu.VMEM((count, rows, model), F32)]
    whole = pl.BlockSpec((rows, model), lambda j: (0, 0))
    if last:
        scratch = [pltpu.VMEM((RING, RING, half, model), BF16)] + scratch
        out_specs = [pl.BlockSpec((2, 2, half, model), lambda j: (0, 0, 0, 0))] * RING
        out_shape = [jax.ShapeDtypeStruct((2, 2, half, model), BF16)] * RING
    else:
        out_specs = [whole] * count
        out_shape = [jax.ShapeDtypeStruct((rows, model), BF16)] * count
    return pl.pallas_call(
        kernel,
        grid=(steps,),
        in_specs=([pl.BlockSpec(memory_space=pltpu.SMEM)] if last else [])
        + [pl.BlockSpec((2, rows, tile), lambda j: (0, 0, j))] * (2 * count)
        + [pl.BlockSpec((model, tile), lambda j: (0, j))] * 4
        + [whole] * len(ready),
        out_specs=out_specs,
        out_shape=out_shape,
        scratch_shapes=scratch,
        compiler_params=params(16),
        cost_estimate=cost(
            8 * count * rows * model * width, 8 * model * width + 8 * count * rows * width
        ),
        name="input_products",
    )(*([place] if last else []), *own, *other, *weights, *ready)


def on_device(layer_input, gate_pre, up_pre, grad_out, w_gate, w_up, w_down):
    x, y, z, core = (lax.axis_index(name) for name in ("x", "y", "z", "c"))
    place = jnp.stack([x, y, z, core]).astype(jnp.int32)
    rows, width = gate_pre.shape
    half, model = rows // 2, w_down.shape[1]

    both = jnp.concatenate([grad_out, layer_input], 1)
    both = lax.all_gather(both, ("z", "c"), axis=0, tiled=True)

    def half_of_tokens(value, shape):
        halves = value.reshape(shape)
        return jnp.stack([pick(halves, core, 1), swap(pick(halves, 1 - core, 1))])

    gate_val, up_val = gate_pre.astype(F32), up_pre.astype(F32)
    hidden = (gate_val * jax.nn.sigmoid(gate_val) * up_val).astype(BF16)
    hid_own, hid_other = first_gather(half_of_tokens(hidden, (1, 2, half, width)))
    hid_own_after, hid_other_before = mix(hid_own, 2, -1), mix(hid_other, 2, 1)
    hid_own_before, hid_other_after = mix(hid_own, 2, 1), mix(hid_other, 2, -1)

    tokens, tokens_theirs = travel_order(place, both[:, :model])
    w_down_other, w_gate_other, w_up_other = swap(w_down), swap(w_gate), swap(w_up)

    def hidden_across(sums):
        return (
            mix(tie(hid_other_before, sums), 2, 1),
            mix(tie(hid_own_after, sums), 2, -1),
        )

    grad_hidden, (hid_other_across, hid_own_across) = scatter_sum(
        tokens,
        w_down,
        w_down_other,
        (hid_own_after, hid_other_before, hid_own_before, hid_other_after)
        + (w_gate_other, w_up_other),
        hidden_across,
    )

    gate_val = half_of_tokens(gate_pre, (1, 2, half, width))[:, 0].astype(F32)
    up_val = half_of_tokens(up_pre, (1, 2, half, width))[:, 0].astype(F32)
    sigmoid_val = jax.nn.sigmoid(gate_val)
    gate_grad = grad_hidden * up_val * sigmoid_val * (1.0 + gate_val * (1.0 - sigmoid_val))
    up_grad = grad_hidden * (gate_val * sigmoid_val)
    own, other = first_gather(jnp.stack([gate_grad, up_grad], 1).astype(BF16))

    own_after, other_before = mix(own, 2, -1), mix(other, 2, 1)
    own_before, other_after = mix(own, 2, 1), mix(other, 2, -1)

    (grad_down,) = weight_grads(
        tokens,
        tokens_theirs,
        [hid_own, hid_own_after, hid_own_across, hid_own_before],
        [swap(p) for p in (hid_other, hid_other_after, hid_other_across, hid_other_before)],
        flip=True,
    )
    input_mine, input_theirs = travel_order(place, tie(both, own)[:, model:])
    own_after, other_before, own_before, other_after, grad_down, *_ = lax.optimization_barrier(
        (own_after, other_before, own_before, other_after, grad_down, input_mine)
    )
    other_across, own_across = mix(other_before, 2, 1), mix(own_after, 2, -1)

    weights = (w_gate, w_up, w_gate_other, w_up_other)
    ready = input_products(
        [own, own_after, own_before],
        [other, other_after, other_before],
        weights,
    )
    theirs = [swap(p) for p in (other, other_after, other_before)]
    own_across, other_across, *ready = lax.optimization_barrier(
        (own_across, other_across, *ready, *theirs)
    )[:5]
    parts = input_products([own_across], [other_across], weights, ready, place)
    grad_gate, grad_up = weight_grads(
        input_mine,
        input_theirs,
        [own, own_after, own_across, own_before],
        [theirs[0], theirs[1], swap(other_across), theirs[2]],
    )
    received = [along_z(parts[k], step) for k, step in ((1, 1), (3, -1), (2, 2))]
    total = tie(parts[0], grad_gate, grad_up).astype(F32)
    for part in received:
        total = total + part.astype(F32)
    total = total.astype(BF16)
    keep, got = total[0], swap(total[1])
    grad_input = jnp.where(
        core == 0, jnp.stack([keep, got], 1), jnp.stack([got, keep], 1)
    ).reshape(4 * half, model)

    return grad_input, grad_gate, grad_up, grad_down


def solution(mesh):
    chips = Mesh(mesh.devices.reshape(RING, RING, RING, 2), ("x", "y", "z", "c"))
    row, col = ("x", "y"), ("z", "c")
    in_specs = (
        P(col, row),
        P(row, col),
        P(row, col),
        P(col, row),
        P(row, col),
        P(row, col),
        P(col, row),
    )
    out_specs = (P(col, row), P(row, col), P(row, col), P(col, row))
    return jax.shard_map(
        on_device, mesh=chips, in_specs=in_specs, out_specs=out_specs, check_vma=False
    )
```

```python
import jax
import jax.numpy as jnp
from jax import lax
from jax.experimental import pallas as pl
from jax.experimental.pallas import tpu as pltpu
from jax.sharding import Mesh, PartitionSpec as P

F32 = jnp.float32
BF16 = jnp.bfloat16
RING = 4
LAST = (((1,), (1,)), ((), ()))
FIRST = (((0,), (0,)), ((), ()))
MIB = 2**20


def mix(value, phase, step):
    pairs = []
    for x in range(RING):
        for y in range(RING):
            for core in range(2):
                if (core == 0) == (phase == 1):
                    to = ((x + step) % RING, y)
                else:
                    to = (x, (y + step) % RING)
                pairs.append(((x * RING + y) * 2 + core, (to[0] * RING + to[1]) * 2 + core))
    return lax.ppermute(value, ("x", "y", "c"), pairs)


def along_z(value, step):
    return lax.ppermute(value, "z", [(z, (z + step) % RING) for z in range(RING)])


def swap(value):
    return lax.ppermute(value, "c", [(0, 1), (1, 0)])


def pick(value, at, axis=0):
    return lax.dynamic_index_in_dim(value, at, axis, keepdims=False)


def tie(value, *after):
    return lax.optimization_barrier((value, *after))[0]


def params(mebibytes):
    return pltpu.CompilerParams(vmem_limit_bytes=mebibytes * MIB)


def light():
    return pl.CostEstimate(flops=1, bytes_accessed=1, transcendentals=0)


def travel_order(place, value, part, flip=False):
    tokens, model = value.shape[0], value.shape[1] // 2
    half = tokens // 32
    value = value.reshape(RING, RING, 2, half, 2 * model)

    def kernel(place_ref, value_ref, *results):
        x, y, core = place_ref[0], place_ref[1], place_ref[3]
        for i, owner in enumerate((core, 1 - core)):
            for second in range(RING):
                block = []
                for first in range(RING):
                    at_x = lax.rem(x + jnp.where(owner == 0, first, second), RING)
                    at_y = lax.rem(y + jnp.where(owner == 0, second, first), RING)
                    block.append(value_ref[at_x, at_y, owner])
                block = jnp.concatenate(block, 0)
                if flip:
                    at = (i * RING + second) * RING * half
                    results[0][:, at : at + RING * half] = block.T
                else:
                    results[i][second] = block

    shape, count = ((model, tokens), 1) if flip else ((RING, RING * half, model), 2)
    return pl.pallas_call(
        kernel,
        grid=(1,),
        in_specs=[
            pl.BlockSpec(memory_space=pltpu.SMEM),
            pl.BlockSpec((RING, RING, 2, half, model), lambda j: (0, 0, 0, 0, part)),
        ],
        out_specs=[pl.BlockSpec(shape, lambda j: (0,) * len(shape))] * count,
        out_shape=[jax.ShapeDtypeStruct(shape, BF16)] * count,
        compiler_params=params(12),
        cost_estimate=light(),
        name="travel_order",
    )(place, value)


def down_products(tokens, groups):
    _, rows, model = tokens.shape
    parts = [part for group in groups for part in group]
    width = parts[0][1].shape[0]
    tile = width // 2
    operands, in_specs = [], []
    for k, weight, extras in parts:
        operands += [tokens, weight] + [stack for stack, _ in extras]
        in_specs.append(pl.BlockSpec((1, rows, model), lambda j, k=k: (k, 0, 0)))
        in_specs.append(pl.BlockSpec((tile, model), lambda j: (j, 0)))
        for _, at in extras:
            in_specs.append(pl.BlockSpec((1, rows, tile), lambda j, at=at: (at, 0, j)))

    def kernel(*refs):
        at = 0
        for out, group in zip(refs[len(operands) :], groups):
            for n, (_, _, extras) in enumerate(group):
                total = lax.dot_general(
                    refs[at][0], refs[at + 1][...], LAST, preferred_element_type=F32
                )
                for i in range(len(extras)):
                    total = total + refs[at + 2 + i][0].astype(F32)
                at += 2 + len(extras)
                out[n] = total.astype(BF16)

    return pl.pallas_call(
        kernel,
        grid=(2,),
        in_specs=in_specs,
        out_specs=[pl.BlockSpec((len(group), rows, tile), lambda j: (0, 0, j)) for group in groups],
        out_shape=[jax.ShapeDtypeStruct((len(group), rows, width), BF16) for group in groups],
        compiler_params=params(14),
        cost_estimate=light(),
        name="down_products",
    )(*operands)


def scatter_sum(tokens, weight, weight_other, before, between, beside):
    (fwd,) = down_products(tokens, [[(2, weight, ()), (1, weight_other, ())]])
    (back,) = down_products(tokens, [[(2, weight_other, ()), (3, weight, ())]])
    fwd, back, *_ = lax.optimization_barrier((fwd, back, *before))
    fwd, back = mix(fwd, 2, 1), mix(back, 2, -1)
    moved = between()
    own, other = down_products(
        tokens, [[(1, weight, ((fwd, 0),))], [(3, weight_other, ((back, 0),))]]
    )
    own, other = mix(own, 2, 1), mix(other, 2, -1)
    (sums,) = down_products(
        tie(tokens, *moved),
        [
            [
                (0, weight, ((own, 0), (back, 1))),
                (0, weight_other, ((fwd, 1), (other, 0))),
            ]
        ],
    )
    sums = sums.reshape(2, RING, -1, sums.shape[-1])
    done = beside(sums, *moved)
    total = tie(sums[:, 0], *done).astype(F32)
    for distance, step in ((2, 2), (1, 1), (3, -1)):
        total = total + mix(sums[:, distance], 1, step).astype(F32)
    return total, moved, done


def first_gather(block):
    _, n, half, width = block.shape
    across, after, before = mix(block, 1, 2), mix(block, 1, -1), mix(block, 1, 1)
    return tuple(
        jnp.stack([piece[i] for piece in (block, after, across, before)], 1).reshape(
            n, RING * half, width
        )
        for i in range(2)
    )


def weight_grads(left, mine, theirs, flip=False):
    n, rows, width = mine[0].shape
    ready = len(left) == 1
    model = left[0].shape[0] if ready else left[0].shape[2]
    places = [0] * RING + ([0] * RING if isinstance(theirs, list) else list(range(RING)))
    pieces = [*mine, *(theirs if isinstance(theirs, list) else [theirs] * RING)]
    tile = 256

    def kernel(*refs):
        left_refs, refs = refs[: len(left)], refs[len(left) :]
        held = left_refs[0]
        if not ready:
            held = refs[-1]

            @pl.when(pl.program_id(0) == 0)
            def _():
                for i, ref in enumerate(left_refs):
                    for k in range(RING):
                        at = (i * RING + k) * rows
                        held[:, at : at + rows] = ref[k].T

        for i in range(n):
            right = jnp.concatenate([ref[i] for ref in refs[: len(pieces)]], 0)
            result = jnp.dot(held[...], right, preferred_element_type=F32)
            refs[len(pieces) + i][...] = result.T if flip else result

    if flip:
        shape, out_spec = (width, model), pl.BlockSpec((tile, model), lambda j: (j, 0))
    else:
        shape, out_spec = (model, width), pl.BlockSpec((model, tile), lambda j: (0, j))
    scratch = [] if ready else [pltpu.VMEM((model, rows * len(pieces)), BF16)]
    return pl.pallas_call(
        kernel,
        grid=(width // tile,),
        in_specs=[pl.BlockSpec(a.shape, lambda j, r=a.ndim: (0,) * r) for a in left]
        + [pl.BlockSpec((n, rows, tile), lambda j, at=at: (at, 0, j)) for at in places],
        out_specs=[out_spec] * n,
        out_shape=[jax.ShapeDtypeStruct(shape, F32)] * n,
        scratch_shapes=scratch,
        compiler_params=params(18 if n > 1 else 14),
        cost_estimate=light(),
        name="weight_grads",
    )(*left, *pieces)


def input_products(groups, ready=(), place=None, whole=True):
    last = place is not None
    terms = [term for group in groups for term in group]
    _, rows, width = terms[0][0].shape
    model = terms[0][1][0][0].shape[-2]
    tile = 256 if len(terms) > 1 else width // 2
    steps = width // tile
    half = rows // RING
    pairs = {id(weights): weights for _, weights in terms}
    order = list(pairs)
    weights = [weight for key in order for weight in pairs[key]]
    inputs = ([place] if last else []) + [piece for piece, _ in terms]
    inputs += [weight for weight, _ in weights] + list(ready)
    count = RING if last else len(groups)

    def kernel(*refs):
        ins, refs = refs[: len(inputs)], refs[len(inputs) :]
        outs, scratch = refs[:count], refs[count:]
        place_ref, ins = (ins[0], ins[1:]) if last else (None, ins)
        weight_refs, ready_refs = ins[len(terms) :][: len(weights)], ins[len(terms) + len(weights) :]
        total = scratch[0]
        step = pl.program_id(0)
        at = 0
        for p, group in enumerate(groups):
            value = None
            for _, own_weights in group:
                pair = 2 * order.index(id(own_weights))
                for i in range(2):
                    term = lax.dot_general(
                        ins[at][i], weight_refs[pair + i][...], LAST, preferred_element_type=F32
                    )
                    value = term if value is None else value + term
                at += 1

            @pl.when(step == 0)
            def _():
                total[p] = value

            @pl.when((step > 0) & (step < steps - 1))
            def _():
                total[p] += value

            @pl.when(step == steps - 1)
            def _():
                result = total[p] + value
                if not last:
                    outs[p][...] = result.astype(outs[p].dtype)
                    return
                held = scratch[1]
                x, y, z, core = (place_ref[i] for i in range(4))
                held[2] = (result + ready_refs[0][...]).astype(BF16).reshape(RING, half, model)
                for k, ref in zip((0, 1, 3), ready_refs[1:]):
                    held[k] = ref[...].reshape(RING, half, model)
                for distance in range(RING):
                    at_x = lax.rem(z + distance - x + RING, RING)
                    for j in range(2):
                        for low in range(2):
                            at_y = lax.rem(2 * lax.rem(core + j, 2) + low - y + RING, RING)
                            second = jnp.where(core == 0, at_y, at_x)
                            first = jnp.where(core == 0, at_x, at_y)
                            outs[distance][j, low] = held[second, first]

    scratch = [pltpu.VMEM((len(groups), rows, model), F32)]
    block = pl.BlockSpec((rows, model), lambda j: (0, 0))
    if last:
        scratch.append(pltpu.VMEM((RING, RING, half, model), BF16))
        out_specs = [pl.BlockSpec((2, 2, half, model), lambda j: (0, 0, 0, 0))] * RING
        out_shape = [jax.ShapeDtypeStruct((2, 2, half, model), BF16)] * RING
    else:
        out_specs = [block] * count
        out_shape = [jax.ShapeDtypeStruct((rows, model), BF16 if whole else F32)] * count
    return pl.pallas_call(
        kernel,
        grid=(steps,),
        in_specs=([pl.BlockSpec(memory_space=pltpu.SMEM)] if last else [])
        + [pl.BlockSpec((2, rows, tile), lambda j: (0, 0, j))] * len(terms)
        + [
            pl.BlockSpec((model, tile), lambda j: (0, j))
            if at is None
            else pl.BlockSpec((None, model, tile), lambda j, at=at: (at, 0, j))
            for _, at in weights
        ]
        + [block] * len(ready),
        out_specs=out_specs,
        out_shape=out_shape,
        scratch_shapes=scratch,
        compiler_params=params(16),
        cost_estimate=light(),
        name="input_products",
    )(*inputs)


def on_device(layer_input, gate_pre, up_pre, grad_out, w_gate, w_up, w_down):
    x, y, z, core = (lax.axis_index(name) for name in ("x", "y", "z", "c"))
    place = jnp.stack([x, y, z, core]).astype(jnp.int32)
    rows, width = gate_pre.shape
    half, model = rows // 2, w_down.shape[1]

    def half_of_tokens(value, shape):
        halves = value.reshape(shape)
        return jnp.stack([pick(halves, core, 1), swap(pick(halves, 1 - core, 1))])

    gate_val, up_val = gate_pre.astype(F32), up_pre.astype(F32)
    hidden = (gate_val * jax.nn.sigmoid(gate_val) * up_val).astype(BF16)
    both = jnp.concatenate([tie(grad_out, hidden), layer_input], 1)
    both = lax.all_gather(both, ("z", "c"), axis=0, tiled=True)
    hid_own, hid_other = first_gather(half_of_tokens(hidden, (1, 2, half, width)))
    w_down_other = swap(w_down)
    hid_own, hid_other, w_down_other = lax.optimization_barrier((hid_own, hid_other, w_down_other))
    hid_own_after, hid_other_before = mix(hid_own, 2, -1), mix(hid_other, 2, 1)
    hid_own_before, hid_other_after = mix(hid_own, 2, 1), mix(hid_other, 2, -1)

    tokens, tokens_theirs = travel_order(place, both, 0)
    pre = half_of_tokens(jnp.stack([gate_pre, up_pre]), (2, 2, half, width))

    def hidden_across():
        return mix(hid_other_before, 2, 1), mix(hid_own_after, 2, -1)

    def hidden_swap(sums, other_across, own_across):
        pieces = [hid_other, hid_other_after, other_across, hid_other_before]
        return (swap(tie(jnp.concatenate(pieces), sums)),)

    grad_hidden, (_, hid_own_across), (hid_theirs,) = scatter_sum(
        tokens,
        w_down,
        w_down_other,
        (hid_own_after, hid_other_before, hid_own_before, hid_other_after, pre),
        hidden_across,
        hidden_swap,
    )

    gate_val, up_val = pre[:, 0].astype(F32), pre[:, 1].astype(F32)
    sigmoid_val = jax.nn.sigmoid(gate_val)
    gate_grad = grad_hidden * up_val * sigmoid_val * (1.0 + gate_val * (1.0 - sigmoid_val))
    up_grad = grad_hidden * (gate_val * sigmoid_val)
    own, other = first_gather(jnp.stack([gate_grad, up_grad], 1).astype(BF16))

    w_other = swap(tie(jnp.stack([w_gate, w_up]), grad_hidden))
    own, other, w_other = lax.optimization_barrier((own, other, w_other))
    own_after, other_before = mix(own, 2, -1), mix(other, 2, 1)

    (grad_down,) = weight_grads(
        (tokens, tokens_theirs),
        [hid_own, hid_own_after, hid_own_across, hid_own_before],
        hid_theirs,
        flip=True,
    )
    (input_left,) = travel_order(place, tie(both, own), 1, flip=True)
    theirs = [swap(other)]
    own_before, other_after = mix(own, 2, 1), mix(other, 2, -1)
    own_after, other_before, *_ = lax.optimization_barrier(
        (own_after, other_before, input_left, grad_down, theirs[0])
    )
    other_across, own_across = mix(other_before, 2, 1), mix(own_after, 2, -1)

    here, there = ((w_gate, None), (w_up, None)), ((w_other, 0), (w_other, 1))
    ready = input_products(
        [
            [(own, here), (other, there)],
            [(own_after, here), (other_after, there)],
            [(own_before, here), (other_before, there)],
        ]
    )
    other_across, *ready, theirs_before = lax.optimization_barrier(
        (other_across, *ready, swap(other_before))
    )
    theirs += [swap(other_after), swap(other_across), theirs_before]
    (first,) = input_products([[(other_across, there)]], whole=False)
    parts = input_products([[(own_across, here)]], [first, *ready], place)
    grad_gate, grad_up = weight_grads(
        (input_left,),
        [own, own_after, own_across, own_before],
        theirs,
    )
    received = [along_z(parts[k], step) for k, step in ((2, 2), (1, 1), (3, -1))]
    total = tie(parts[0], grad_gate, grad_up).astype(F32)
    for part in received:
        total = total + part.astype(F32)
    total = total.astype(BF16)
    keep, got = total[0], swap(total[1])
    grad_input = jnp.where(
        core == 0, jnp.stack([keep, got], 1), jnp.stack([got, keep], 1)
    ).reshape(4 * half, model)

    return grad_input, grad_gate, grad_up, grad_down


def solution(mesh):
    chips = Mesh(mesh.devices.reshape(RING, RING, RING, 2), ("x", "y", "z", "c"))
    row, col = ("x", "y"), ("z", "c")
    in_specs = (
        P(col, row),
        P(row, col),
        P(row, col),
        P(col, row),
        P(row, col),
        P(row, col),
        P(col, row),
    )
    out_specs = (P(col, row), P(row, col), P(row, col), P(col, row))
    return jax.shard_map(
        on_device, mesh=chips, in_specs=in_specs, out_specs=out_specs, check_vma=False
    )
```

```python
import jax
import jax.numpy as jnp
from jax import lax
from jax.experimental import pallas as pl
from jax.experimental.pallas import tpu as pltpu
from jax.sharding import Mesh, PartitionSpec as P

F32 = jnp.float32
BF16 = jnp.bfloat16
RING = 4
LAST = (((1,), (1,)), ((), ()))
FIRST = (((0,), (0,)), ((), ()))
MIB = 2**20


def mix(value, phase, step):
    pairs = []
    for x in range(RING):
        for y in range(RING):
            for core in range(2):
                if (core == 0) == (phase == 1):
                    to = ((x + step) % RING, y)
                else:
                    to = (x, (y + step) % RING)
                pairs.append(((x * RING + y) * 2 + core, (to[0] * RING + to[1]) * 2 + core))
    return lax.ppermute(value, ("x", "y", "c"), pairs)


def along_z(value, step):
    return lax.ppermute(value, "z", [(z, (z + step) % RING) for z in range(RING)])


def swap(value):
    return lax.ppermute(value, "c", [(0, 1), (1, 0)])


def pick(value, at, axis=0):
    return lax.dynamic_index_in_dim(value, at, axis, keepdims=False)


def tie(value, *after):
    return lax.optimization_barrier((value, *after))[0]


def params(mebibytes):
    return pltpu.CompilerParams(vmem_limit_bytes=mebibytes * MIB)


def light():
    return pl.CostEstimate(flops=1, bytes_accessed=1, transcendentals=0)


def travel_order(place, own, other, flip=False):
    _, rows, model = own.shape
    half = rows // 4
    own, other = (value.reshape(RING, 2, 2, half, model) for value in (own, other))

    def kernel(place_ref, own_ref, other_ref, result, *held):
        x, y, z, core = (place_ref[i] for i in range(4))
        target = held[0] if flip else result
        for side, ref in enumerate((own_ref, other_ref)):
            for step in range(RING):
                at_x = lax.rem(z + step - x + RING, RING)
                for low in range(2):
                    at_y = lax.rem(2 * lax.rem(core + side, 2) + low - y + RING, RING)
                    for owner in range(2):
                        second, first = (at_y, at_x) if owner == 0 else (at_x, at_y)
                        target[lax.rem(core + owner, 2), second, first] = ref[step, low, owner]
        if flip:
            for i in range(2 * RING):
                block = target[i // RING, i % RING].reshape(RING * half, model)
                result[:, i * RING * half : (i + 1) * RING * half] = block.T

    order = (2, RING, RING, half, model)
    shape = (model, 2 * RING * RING * half) if flip else order
    block = pl.BlockSpec((RING, 2, 2, half, model), lambda j: (0,) * 5)
    result = pl.pallas_call(
        kernel,
        grid=(1,),
        in_specs=[pl.BlockSpec(memory_space=pltpu.SMEM), block, block],
        out_specs=pl.BlockSpec(shape, lambda j: (0,) * len(shape)),
        out_shape=jax.ShapeDtypeStruct(shape, BF16),
        scratch_shapes=[pltpu.VMEM(order, BF16)] if flip else [],
        compiler_params=params(16),
        cost_estimate=light(),
        name="travel_order",
    )(place, own, other)
    return result if flip else result.reshape(2, RING, RING * half, model)


def down_products(tokens, groups):
    _, _, rows, model = tokens.shape
    parts = [part for group in groups for part in group]
    width = parts[0][1].shape[0]
    tile = width // 2
    operands, in_specs = [], []
    for k, weight, extras in parts:
        operands += [tokens, weight] + [stack for stack, _ in extras]
        in_specs.append(pl.BlockSpec((None, 1, rows, model), lambda j, k=k: (0, k, 0, 0)))
        in_specs.append(pl.BlockSpec((tile, model), lambda j: (j, 0)))
        for _, at in extras:
            in_specs.append(pl.BlockSpec((1, rows, tile), lambda j, at=at: (at, 0, j)))

    def kernel(*refs):
        at = 0
        for out, group in zip(refs[len(operands) :], groups):
            for n, (_, _, extras) in enumerate(group):
                total = lax.dot_general(
                    refs[at][0], refs[at + 1][...], LAST, preferred_element_type=F32
                )
                for i in range(len(extras)):
                    total = total + refs[at + 2 + i][0].astype(F32)
                at += 2 + len(extras)
                out[n] = total.astype(BF16)

    return pl.pallas_call(
        kernel,
        grid=(2,),
        in_specs=in_specs,
        out_specs=[pl.BlockSpec((len(group), rows, tile), lambda j: (0, 0, j)) for group in groups],
        out_shape=[jax.ShapeDtypeStruct((len(group), rows, width), BF16) for group in groups],
        compiler_params=params(14),
        cost_estimate=light(),
        name="down_products",
    )(*operands)


def scatter_sum(tokens, weight, weight_other, before, between, beside):
    (fwd,) = down_products(tokens, [[(2, weight, ()), (1, weight_other, ())]])
    (back,) = down_products(tokens, [[(2, weight_other, ()), (3, weight, ())]])
    fwd, back, *_ = lax.optimization_barrier((fwd, back, *before))
    fwd, back = mix(fwd, 2, 1), mix(back, 2, -1)
    moved = between()
    own, other = down_products(
        tokens, [[(1, weight, ((fwd, 0),))], [(3, weight_other, ((back, 0),))]]
    )
    own, other = mix(own, 2, 1), mix(other, 2, -1)
    (sums,) = down_products(
        tie(tokens, *moved),
        [
            [
                (0, weight, ((own, 0), (back, 1))),
                (0, weight_other, ((fwd, 1), (other, 0))),
            ]
        ],
    )
    sums = sums.reshape(2, RING, -1, sums.shape[-1])
    done = beside(sums, *moved)
    total = tie(sums[:, 0], *done).astype(F32)
    for distance, step in ((2, 2), (1, 1), (3, -1)):
        total = total + mix(sums[:, distance], 1, step).astype(F32)
    return total, moved, done


def first_gather(block):
    _, n, half, width = block.shape
    across, after, before = mix(block, 1, 2), mix(block, 1, -1), mix(block, 1, 1)
    return tuple(
        jnp.stack([piece[i] for piece in (block, after, across, before)], 1).reshape(
            n, RING * half, width
        )
        for i in range(2)
    )


def weight_grads(left, mine, theirs, flip=False):
    stacked = not isinstance(theirs, list)
    n, (_, rows, width) = (1, theirs.shape) if stacked else (mine[0].shape[0], mine[0].shape)
    ready = left.ndim == 2
    model = left.shape[0] if ready else left.shape[-1]
    if stacked:
        places = [at for _, at in mine] + list(range(RING))
        pieces = [stack for stack, _ in mine] + [theirs] * RING
    else:
        places, pieces = [0] * (2 * RING), [*mine, *theirs]
    tile = 256

    def kernel(left_ref, *refs):
        held = left_ref
        if not ready:
            held = refs[-1]

            @pl.when(pl.program_id(0) == 0)
            def _():
                for i in range(2 * RING):
                    held[:, i * rows : (i + 1) * rows] = left_ref[i // RING, i % RING].T

        for i in range(n):
            right = jnp.concatenate([ref[i] for ref in refs[: len(pieces)]], 0)
            result = jnp.dot(held[...], right, preferred_element_type=F32)
            refs[len(pieces) + i][...] = result.T if flip else result

    if flip:
        shape, out_spec = (width, model), pl.BlockSpec((tile, model), lambda j: (j, 0))
    else:
        shape, out_spec = (model, width), pl.BlockSpec((model, tile), lambda j: (0, j))
    scratch = [] if ready else [pltpu.VMEM((model, rows * len(pieces)), BF16)]
    return pl.pallas_call(
        kernel,
        grid=(width // tile,),
        in_specs=[pl.BlockSpec(left.shape, lambda j: (0,) * left.ndim)]
        + [pl.BlockSpec((n, rows, tile), lambda j, at=at: (at, 0, j)) for at in places],
        out_specs=[out_spec] * n,
        out_shape=[jax.ShapeDtypeStruct(shape, F32)] * n,
        scratch_shapes=scratch,
        compiler_params=params(18 if n > 1 else 14),
        cost_estimate=light(),
        name="weight_grads",
    )(left, *pieces)


def input_products(groups, ready=(), place=None, whole=True):
    last = place is not None
    terms = [term for group in groups for term in group]
    _, rows, width = terms[0][0].shape
    model = terms[0][1][0][0].shape[-2]
    tile = 256 if len(terms) > 1 else width // 2
    steps = width // tile
    half = rows // RING
    pairs = {id(weights): weights for _, weights in terms}
    order = list(pairs)
    weights = [weight for key in order for weight in pairs[key]]
    inputs = ([place] if last else []) + [piece for piece, _ in terms]
    inputs += [weight for weight, _ in weights] + list(ready)
    count = RING if last else len(groups)

    def kernel(*refs):
        ins, refs = refs[: len(inputs)], refs[len(inputs) :]
        outs, scratch = refs[:count], refs[count:]
        place_ref, ins = (ins[0], ins[1:]) if last else (None, ins)
        weight_refs, ready_refs = ins[len(terms) :][: len(weights)], ins[len(terms) + len(weights) :]
        total = scratch[0]
        step = pl.program_id(0)
        at = 0
        for p, group in enumerate(groups):
            value = None
            for _, own_weights in group:
                pair = 2 * order.index(id(own_weights))
                for i in range(2):
                    term = lax.dot_general(
                        ins[at][i], weight_refs[pair + i][...], LAST, preferred_element_type=F32
                    )
                    value = term if value is None else value + term
                at += 1

            @pl.when(step == 0)
            def _():
                total[p] = value

            @pl.when((step > 0) & (step < steps - 1))
            def _():
                total[p] += value

            @pl.when(step == steps - 1)
            def _():
                result = total[p] + value
                if not last:
                    outs[p][...] = result.astype(outs[p].dtype)
                    return
                held = scratch[1]
                x, y, z, core = (place_ref[i] for i in range(4))
                held[2] = (result + ready_refs[0][...]).astype(BF16).reshape(RING, half, model)
                for k, ref in zip((0, 1, 3), ready_refs[1:]):
                    held[k] = ref[...].reshape(RING, half, model)
                for distance in range(RING):
                    at_x = lax.rem(z + distance - x + RING, RING)
                    for j in range(2):
                        for low in range(2):
                            at_y = lax.rem(2 * lax.rem(core + j, 2) + low - y + RING, RING)
                            second = jnp.where(core == 0, at_y, at_x)
                            first = jnp.where(core == 0, at_x, at_y)
                            outs[distance][j, low] = held[second, first]

    scratch = [pltpu.VMEM((len(groups), rows, model), F32)]
    block = pl.BlockSpec((rows, model), lambda j: (0, 0))
    if last:
        scratch.append(pltpu.VMEM((RING, RING, half, model), BF16))
        out_specs = [pl.BlockSpec((2, 2, half, model), lambda j: (0, 0, 0, 0))] * RING
        out_shape = [jax.ShapeDtypeStruct((2, 2, half, model), BF16)] * RING
    else:
        out_specs = [block] * count
        out_shape = [jax.ShapeDtypeStruct((rows, model), BF16 if whole else F32)] * count
    return pl.pallas_call(
        kernel,
        grid=(steps,),
        in_specs=([pl.BlockSpec(memory_space=pltpu.SMEM)] if last else [])
        + [pl.BlockSpec((2, rows, tile), lambda j: (0, 0, j))] * len(terms)
        + [
            pl.BlockSpec((model, tile), lambda j: (0, j))
            if at is None
            else pl.BlockSpec((None, model, tile), lambda j, at=at: (at, 0, j))
            for _, at in weights
        ]
        + [block] * len(ready),
        out_specs=out_specs,
        out_shape=out_shape,
        scratch_shapes=scratch,
        compiler_params=params(16),
        cost_estimate=light(),
        name="input_products",
    )(*inputs)


def on_device(layer_input, gate_pre, up_pre, grad_out, w_gate, w_up, w_down):
    x, y, z, core = (lax.axis_index(name) for name in ("x", "y", "z", "c"))
    place = jnp.stack([x, y, z, core]).astype(jnp.int32)
    rows, width = gate_pre.shape
    half, model = rows // 2, w_down.shape[1]

    def half_of_tokens(value, shape):
        halves = value.reshape(shape)
        return jnp.stack([pick(halves, core, 1), swap(pick(halves, 1 - core, 1))])

    gate_val, up_val = gate_pre.astype(F32), up_pre.astype(F32)
    hidden = (gate_val * jax.nn.sigmoid(gate_val) * up_val).astype(BF16)
    def from_z(value):
        return jnp.stack([value, along_z(value, -1), along_z(value, 2), along_z(value, 1)])

    hidden = half_of_tokens(hidden, (1, 2, half, width))
    hid = jnp.concatenate(first_gather(hidden))
    w_down_other = swap(tie(w_down, hidden))
    hid, w_down_other = lax.optimization_barrier((hid, w_down_other))
    hid_after, hid_before = mix(hid, 2, -1), mix(hid, 2, 1)

    out_blocks = from_z(tie(grad_out, hidden))
    tokens = travel_order(place, out_blocks, swap(out_blocks))
    pre = half_of_tokens(jnp.stack([gate_pre, up_pre]), (2, 2, half, width))

    def hidden_across():
        return mix(hid_before[1], 2, 1), mix(hid_after[0], 2, -1)

    def hidden_swap(sums, other_across, own_across):
        pieces = jnp.stack([hid[1], hid_after[1], other_across, hid_before[1]])
        return (swap(tie(pieces, sums)),)

    grad_hidden, (_, hid_own_across), (hid_theirs,) = scatter_sum(
        tokens,
        w_down,
        w_down_other,
        (hid_after, hid_before, pre),
        hidden_across,
        hidden_swap,
    )

    gate_val, up_val = pre[:, 0].astype(F32), pre[:, 1].astype(F32)
    sigmoid_val = jax.nn.sigmoid(gate_val)
    gate_grad = grad_hidden * up_val * sigmoid_val * (1.0 + gate_val * (1.0 - sigmoid_val))
    up_grad = grad_hidden * (gate_val * sigmoid_val)
    own, other = first_gather(jnp.stack([gate_grad, up_grad], 1).astype(BF16))

    w_other = swap(tie(jnp.stack([w_gate, w_up]), grad_hidden))
    own, other, w_other = lax.optimization_barrier((own, other, w_other))
    own_after, other_before = mix(own, 2, -1), mix(other, 2, 1)

    (grad_down,) = weight_grads(
        tokens,
        [(hid, 0), (hid_after, 0), (hid_own_across[None], 0), (hid_before, 0)],
        hid_theirs,
        flip=True,
    )
    input_blocks = from_z(tie(layer_input, own))
    own_later, other_later, input_blocks, grad_down = lax.optimization_barrier(
        (own, other, input_blocks, grad_down)
    )
    own_before, other_after = mix(own_later, 2, 1), mix(other_later, 2, -1)
    input_left = travel_order(place, input_blocks, swap(input_blocks), flip=True)
    other_across, own_across = mix(other_before, 2, 1), mix(own_after, 2, -1)

    here, there = ((w_gate, None), (w_up, None)), ((w_other, 0), (w_other, 1))
    ready = input_products(
        [
            [(own, here), (other, there)],
            [(own_after, here), (other_after, there)],
            [(own_before, here), (other_before, there)],
        ]
    )
    other_across, input_left, *ready, theirs_here, theirs_before = lax.optimization_barrier(
        (other_across, input_left, *ready, swap(other_later), swap(other_before))
    )
    theirs = [theirs_here, swap(other_after), swap(other_across), theirs_before]
    (first,) = input_products([[(other_across, there)]], whole=False)
    parts = input_products([[(own_across, here)]], [first, *ready], place)
    grad_gate, grad_up = weight_grads(
        input_left,
        [own, own_after, own_across, own_before],
        theirs,
    )
    received = [along_z(parts[k], step) for k, step in ((2, 2), (1, 1), (3, -1))]
    total = tie(parts[0], grad_gate, grad_up).astype(F32)
    for part in received:
        total = total + part.astype(F32)
    total = total.astype(BF16)
    keep, got = total[0], swap(total[1])
    grad_input = jnp.where(
        core == 0, jnp.stack([keep, got], 1), jnp.stack([got, keep], 1)
    ).reshape(4 * half, model)

    return grad_input, grad_gate, grad_up, grad_down


def solution(mesh):
    chips = Mesh(mesh.devices.reshape(RING, RING, RING, 2), ("x", "y", "z", "c"))
    row, col = ("x", "y"), ("z", "c")
    in_specs = (
        P(col, row),
        P(row, col),
        P(row, col),
        P(col, row),
        P(row, col),
        P(row, col),
        P(col, row),
    )
    out_specs = (P(col, row), P(row, col), P(row, col), P(col, row))
    return jax.shard_map(
        on_device, mesh=chips, in_specs=in_specs, out_specs=out_specs, check_vma=False
    )
```

```python
import jax
import jax.numpy as jnp
from jax import lax
from jax.experimental import pallas as pl
from jax.experimental.pallas import tpu as pltpu
from jax.sharding import Mesh, PartitionSpec as P

F32 = jnp.float32
BF16 = jnp.bfloat16
RING = 4
LAST = (((1,), (1,)), ((), ()))
FIRST = (((0,), (0,)), ((), ()))
MIB = 2**20


def mix(value, phase, step):
    pairs = []
    for x in range(RING):
        for y in range(RING):
            for core in range(2):
                if (core == 0) == (phase == 1):
                    to = ((x + step) % RING, y)
                else:
                    to = (x, (y + step) % RING)
                pairs.append(((x * RING + y) * 2 + core, (to[0] * RING + to[1]) * 2 + core))
    return lax.ppermute(value, ("x", "y", "c"), pairs)


def along_z(value, step):
    return lax.ppermute(value, "z", [(z, (z + step) % RING) for z in range(RING)])


def swap(value):
    return lax.ppermute(value, "c", [(0, 1), (1, 0)])


def pick(value, at, axis=0):
    return lax.dynamic_index_in_dim(value, at, axis, keepdims=False)


def tie(value, *after):
    return lax.optimization_barrier((value, *after))[0]


def params(mebibytes):
    return pltpu.CompilerParams(vmem_limit_bytes=mebibytes * MIB)


def light():
    return pl.CostEstimate(flops=1, bytes_accessed=1, transcendentals=0)


def travel_order(place, own, other, flip=False):
    _, rows, model = own.shape
    half = rows // 4
    own, other = (value.reshape(RING, 2, 2, half, model) for value in (own, other))

    def kernel(place_ref, own_ref, other_ref, result, *held):
        x, y, z, core = (place_ref[i] for i in range(4))
        target = held[0] if flip else result
        for side, ref in enumerate((own_ref, other_ref)):
            for step in range(RING):
                at_x = lax.rem(z + step - x + RING, RING)
                for low in range(2):
                    at_y = lax.rem(2 * lax.rem(core + side, 2) + low - y + RING, RING)
                    for owner in range(2):
                        second, first = (at_y, at_x) if owner == 0 else (at_x, at_y)
                        target[lax.rem(core + owner, 2), second, first] = ref[step, low, owner]
        if flip:
            for i in range(2 * RING):
                block = target[i // RING, i % RING].reshape(RING * half, model)
                result[:, i * RING * half : (i + 1) * RING * half] = block.T

    order = (2, RING, RING, half, model)
    shape = (model, 2 * RING * RING * half) if flip else order
    block = pl.BlockSpec((RING, 2, 2, half, model), lambda j: (0,) * 5)
    result = pl.pallas_call(
        kernel,
        grid=(1,),
        in_specs=[pl.BlockSpec(memory_space=pltpu.SMEM), block, block],
        out_specs=pl.BlockSpec(shape, lambda j: (0,) * len(shape)),
        out_shape=jax.ShapeDtypeStruct(shape, BF16),
        scratch_shapes=[pltpu.VMEM(order, BF16)] if flip else [],
        compiler_params=params(16),
        cost_estimate=light(),
        name="travel_order",
    )(place, own, other)
    return result if flip else result.reshape(2, RING, RING * half, model)


def down_products(tokens, groups):
    _, _, rows, model = tokens.shape
    parts = [part for group in groups for part in group]
    width = parts[0][1].shape[0]
    tile = width // 2
    operands, in_specs = [], []
    for k, weight, extras in parts:
        operands += [tokens, weight] + [stack for stack, _ in extras]
        in_specs.append(pl.BlockSpec((None, 1, rows, model), lambda j, k=k: (0, k, 0, 0)))
        in_specs.append(pl.BlockSpec((tile, model), lambda j: (j, 0)))
        for _, at in extras:
            in_specs.append(pl.BlockSpec((1, rows, tile), lambda j, at=at: (at, 0, j)))

    def kernel(*refs):
        at = 0
        for out, group in zip(refs[len(operands) :], groups):
            for n, (_, _, extras) in enumerate(group):
                total = lax.dot_general(
                    refs[at][0], refs[at + 1][...], LAST, preferred_element_type=F32
                )
                for i in range(len(extras)):
                    total = total + refs[at + 2 + i][0].astype(F32)
                at += 2 + len(extras)
                out[n] = total.astype(BF16)

    return pl.pallas_call(
        kernel,
        grid=(2,),
        in_specs=in_specs,
        out_specs=[pl.BlockSpec((len(group), rows, tile), lambda j: (0, 0, j)) for group in groups],
        out_shape=[jax.ShapeDtypeStruct((len(group), rows, width), BF16) for group in groups],
        compiler_params=params(14),
        cost_estimate=light(),
        name="down_products",
    )(*operands)


def scatter_sum(tokens, weight, weight_other, before, between):
    (fwd,) = down_products(tokens, [[(2, weight, ()), (1, weight_other, ())]])
    (back,) = down_products(tokens, [[(2, weight_other, ()), (3, weight, ())]])
    fwd, back, *_ = lax.optimization_barrier((fwd, back, *before))
    fwd, back = mix(fwd, 2, 1), mix(back, 2, -1)
    own, other = down_products(
        tokens, [[(1, weight, ((fwd, 0),))], [(3, weight_other, ((back, 0),))]]
    )
    moved = between(own, other)
    own, other = mix(own, 2, 1), mix(other, 2, -1)
    (sums,) = down_products(
        tokens,
        [
            [
                (0, weight, ((own, 0), (back, 1))),
                (0, weight_other, ((fwd, 1), (other, 0))),
            ]
        ],
    )
    sums = sums.reshape(2, RING, -1, sums.shape[-1])
    total = tie(sums[:, 0], *moved).astype(F32)
    for distance, step in ((2, 2), (1, 1), (3, -1)):
        total = total + mix(sums[:, distance], 1, step).astype(F32)
    return total, moved


def first_gather(block):
    _, n, half, width = block.shape
    across, after, before = mix(block, 1, 2), mix(block, 1, -1), mix(block, 1, 1)
    return tuple(
        jnp.stack([piece[i] for piece in (block, after, across, before)], 1).reshape(
            n, RING * half, width
        )
        for i in range(2)
    )


def weight_grads(left, mine, theirs, flip=False):
    stacked = not isinstance(theirs, list)
    n, (_, rows, width) = (1, theirs.shape) if stacked else (mine[0].shape[0], mine[0].shape)
    ready = left.ndim == 2
    model = left.shape[0] if ready else left.shape[-1]
    if stacked:
        places = [at for _, at in mine] + list(range(RING))
        pieces = [stack for stack, _ in mine] + [theirs] * RING
    else:
        places, pieces = [0] * (2 * RING), [*mine, *theirs]
    tile = 256

    def kernel(left_ref, *refs):
        held = left_ref
        if not ready:
            held = refs[-1]

            @pl.when(pl.program_id(0) == 0)
            def _():
                for i in range(2 * RING):
                    held[:, i * rows : (i + 1) * rows] = left_ref[i // RING, i % RING].T

        for i in range(n):
            right = jnp.concatenate([ref[i] for ref in refs[: len(pieces)]], 0)
            result = jnp.dot(held[...], right, preferred_element_type=F32)
            refs[len(pieces) + i][...] = result.T if flip else result

    if flip:
        shape, out_spec = (width, model), pl.BlockSpec((tile, model), lambda j: (j, 0))
    else:
        shape, out_spec = (model, width), pl.BlockSpec((model, tile), lambda j: (0, j))
    scratch = [] if ready else [pltpu.VMEM((model, rows * len(pieces)), BF16)]
    return pl.pallas_call(
        kernel,
        grid=(width // tile,),
        in_specs=[pl.BlockSpec(left.shape, lambda j: (0,) * left.ndim)]
        + [pl.BlockSpec((n, rows, tile), lambda j, at=at: (at, 0, j)) for at in places],
        out_specs=[out_spec] * n,
        out_shape=[jax.ShapeDtypeStruct(shape, F32)] * n,
        scratch_shapes=scratch,
        compiler_params=params(18 if n > 1 else 14),
        cost_estimate=light(),
        name="weight_grads",
    )(left, *pieces)


def input_products(groups, ready=(), place=None, whole=True):
    last = place is not None
    terms = [term for group in groups for term in group]
    _, rows, width = terms[0][0].shape
    model = terms[0][1][0][0].shape[-2]
    tile = 256 if len(terms) > 1 else width // 2
    steps = width // tile
    half = rows // RING
    pairs = {id(weights): weights for _, weights in terms}
    order = list(pairs)
    weights = [weight for key in order for weight in pairs[key]]
    inputs = ([place] if last else []) + [piece for piece, _ in terms]
    inputs += [weight for weight, _ in weights] + list(ready)
    count = RING if last else len(groups)

    def kernel(*refs):
        ins, refs = refs[: len(inputs)], refs[len(inputs) :]
        outs, scratch = refs[:count], refs[count:]
        place_ref, ins = (ins[0], ins[1:]) if last else (None, ins)
        weight_refs, ready_refs = ins[len(terms) :][: len(weights)], ins[len(terms) + len(weights) :]
        total = scratch[0]
        step = pl.program_id(0)
        at = 0
        for p, group in enumerate(groups):
            value = None
            for _, own_weights in group:
                pair = 2 * order.index(id(own_weights))
                for i in range(2):
                    term = lax.dot_general(
                        ins[at][i], weight_refs[pair + i][...], LAST, preferred_element_type=F32
                    )
                    value = term if value is None else value + term
                at += 1

            @pl.when(step == 0)
            def _():
                total[p] = value

            @pl.when((step > 0) & (step < steps - 1))
            def _():
                total[p] += value

            @pl.when(step == steps - 1)
            def _():
                result = total[p] + value
                if not last:
                    outs[p][...] = result.astype(outs[p].dtype)
                    return
                held = scratch[1]
                x, y, z, core = (place_ref[i] for i in range(4))
                held[2] = (result + ready_refs[0][...]).astype(BF16).reshape(RING, half, model)
                for k, ref in zip((0, 1, 3), ready_refs[1:]):
                    held[k] = ref[...].reshape(RING, half, model)
                for distance in range(RING):
                    at_x = lax.rem(z + distance - x + RING, RING)
                    for j in range(2):
                        for low in range(2):
                            at_y = lax.rem(2 * lax.rem(core + j, 2) + low - y + RING, RING)
                            second = jnp.where(core == 0, at_y, at_x)
                            first = jnp.where(core == 0, at_x, at_y)
                            outs[distance][j, low] = held[second, first]

    scratch = [pltpu.VMEM((len(groups), rows, model), F32)]
    block = pl.BlockSpec((rows, model), lambda j: (0, 0))
    if last:
        scratch.append(pltpu.VMEM((RING, RING, half, model), BF16))
        out_specs = [pl.BlockSpec((2, 2, half, model), lambda j: (0, 0, 0, 0))] * RING
        out_shape = [jax.ShapeDtypeStruct((2, 2, half, model), BF16)] * RING
    else:
        out_specs = [block] * count
        out_shape = [jax.ShapeDtypeStruct((rows, model), BF16 if whole else F32)] * count
    return pl.pallas_call(
        kernel,
        grid=(steps,),
        in_specs=([pl.BlockSpec(memory_space=pltpu.SMEM)] if last else [])
        + [pl.BlockSpec((2, rows, tile), lambda j: (0, 0, j))] * len(terms)
        + [
            pl.BlockSpec((model, tile), lambda j: (0, j))
            if at is None
            else pl.BlockSpec((None, model, tile), lambda j, at=at: (at, 0, j))
            for _, at in weights
        ]
        + [block] * len(ready),
        out_specs=out_specs,
        out_shape=out_shape,
        scratch_shapes=scratch,
        compiler_params=params(16),
        cost_estimate=light(),
        name="input_products",
    )(*inputs)


def on_device(layer_input, gate_pre, up_pre, grad_out, w_gate, w_up, w_down):
    x, y, z, core = (lax.axis_index(name) for name in ("x", "y", "z", "c"))
    place = jnp.stack([x, y, z, core]).astype(jnp.int32)
    rows, width = gate_pre.shape
    half, model = rows // 2, w_down.shape[1]

    def half_of_tokens(value, shape):
        halves = value.reshape(shape)
        return jnp.stack([pick(halves, core, 1), swap(pick(halves, 1 - core, 1))])

    pre = half_of_tokens(jnp.stack([gate_pre, up_pre]), (2, 2, half, width))
    gate_val, up_val = pre[:, 0].astype(F32), pre[:, 1].astype(F32)
    sigmoid_val = jax.nn.sigmoid(gate_val)
    hidden = (gate_val * sigmoid_val * up_val).astype(BF16)[:, None]
    def from_z(value):
        return jnp.stack([value, along_z(value, -1), along_z(value, 2), along_z(value, 1)])

    hid = jnp.concatenate(first_gather(hidden))
    w_down_other = swap(tie(w_down, hidden))
    hid, w_down_other = lax.optimization_barrier((hid, w_down_other))
    hid_after, hid_before = mix(hid, 2, -1), mix(hid, 2, 1)

    out_blocks = from_z(tie(grad_out, hidden))
    tokens = travel_order(place, out_blocks, swap(out_blocks))

    def hidden_across(*after):
        return mix(tie(hid_before[1], *after), 2, 1), mix(tie(hid_after[0], *after), 2, -1)

    grad_hidden, (hid_other_across, hid_own_across) = scatter_sum(
        tokens, w_down, w_down_other, (hid_after, hid_before), hidden_across
    )
    hid_theirs = jnp.stack([hid[1], hid_after[1], hid_other_across, hid_before[1]])
    hid_theirs = swap(tie(hid_theirs, grad_hidden))

    gate_val, up_val = pre[:, 0].astype(F32), pre[:, 1].astype(F32)
    sigmoid_val = jax.nn.sigmoid(gate_val)
    gate_grad = grad_hidden * up_val * sigmoid_val * (1.0 + gate_val * (1.0 - sigmoid_val))
    up_grad = grad_hidden * (gate_val * sigmoid_val)
    own, other = first_gather(jnp.stack([gate_grad, up_grad], 1).astype(BF16))

    w_other = swap(tie(jnp.stack([w_gate, w_up]), grad_hidden))
    own, other, w_other, hid_theirs = lax.optimization_barrier(
        (own, other, w_other, hid_theirs)
    )
    own_after, other_before = mix(own, 2, -1), mix(other, 2, 1)

    (grad_down,) = weight_grads(
        tokens,
        [(hid, 0), (hid_after, 0), (hid_own_across[None], 0), (hid_before, 0)],
        hid_theirs,
        flip=True,
    )
    input_blocks = from_z(tie(layer_input, own))
    own_later, other_later, input_blocks, grad_down = lax.optimization_barrier(
        (own, other, input_blocks, grad_down)
    )
    own_before, other_after = mix(own_later, 2, 1), mix(other_later, 2, -1)
    input_left = travel_order(place, input_blocks, swap(input_blocks), flip=True)
    other_across, own_across = mix(other_before, 2, 1), mix(own_after, 2, -1)

    here, there = ((w_gate, None), (w_up, None)), ((w_other, 0), (w_other, 1))
    ready = input_products(
        [
            [(own, here), (other, there)],
            [(own_after, here), (other_after, there)],
            [(own_before, here), (other_before, there)],
        ]
    )
    other_across, input_left, *ready, theirs_here, theirs_before = lax.optimization_barrier(
        (other_across, input_left, *ready, swap(other_later), swap(other_before))
    )
    theirs = [theirs_here, swap(other_after), swap(other_across), theirs_before]
    (first,) = input_products([[(other_across, there)]], whole=False)
    parts = input_products([[(own_across, here)]], [first, *ready], place)
    grad_gate, grad_up = weight_grads(
        input_left,
        [own, own_after, own_across, own_before],
        theirs,
    )
    received = [along_z(parts[k], step) for k, step in ((2, 2), (1, 1), (3, -1))]
    total = tie(parts[0], grad_gate, grad_up).astype(F32)
    for part in received:
        total = total + part.astype(F32)
    total = total.astype(BF16)
    keep, got = total[0], swap(total[1])
    grad_input = jnp.where(
        core == 0, jnp.stack([keep, got], 1), jnp.stack([got, keep], 1)
    ).reshape(4 * half, model)

    return grad_input, grad_gate, grad_up, grad_down


def solution(mesh):
    chips = Mesh(mesh.devices.reshape(RING, RING, RING, 2), ("x", "y", "z", "c"))
    row, col = ("x", "y"), ("z", "c")
    in_specs = (
        P(col, row),
        P(row, col),
        P(row, col),
        P(col, row),
        P(row, col),
        P(row, col),
        P(col, row),
    )
    out_specs = (P(col, row), P(row, col), P(row, col), P(col, row))
    return jax.shard_map(
        on_device, mesh=chips, in_specs=in_specs, out_specs=out_specs, check_vma=False
    )
```

```python
import jax
import jax.numpy as jnp
from jax import lax
from jax.experimental import pallas as pl
from jax.experimental.pallas import tpu as pltpu
from jax.sharding import Mesh, PartitionSpec as P

F32 = jnp.float32
BF16 = jnp.bfloat16
RING = 4
LAST = (((1,), (1,)), ((), ()))
FIRST = (((0,), (0,)), ((), ()))
MIB = 2**20


def mix(value, phase, step):
    pairs = []
    for x in range(RING):
        for y in range(RING):
            for core in range(2):
                if (core == 0) == (phase == 1):
                    to = ((x + step) % RING, y)
                else:
                    to = (x, (y + step) % RING)
                pairs.append(((x * RING + y) * 2 + core, (to[0] * RING + to[1]) * 2 + core))
    return lax.ppermute(value, ("x", "y", "c"), pairs)


def along_z(value, step):
    return lax.ppermute(value, "z", [(z, (z + step) % RING) for z in range(RING)])


def swap(value):
    return lax.ppermute(value, "c", [(0, 1), (1, 0)])


def pick(value, at, axis=0):
    return lax.dynamic_index_in_dim(value, at, axis, keepdims=False)


def tie(value, *after):
    return lax.optimization_barrier((value, *after))[0]


def params(mebibytes):
    return pltpu.CompilerParams(vmem_limit_bytes=mebibytes * MIB)


def light():
    return pl.CostEstimate(flops=1, bytes_accessed=1, transcendentals=0)


def travel_order(place, own, other, flip=False):
    _, rows, model = own.shape
    half = rows // 4
    own, other = (value.reshape(RING, 2, 2, half, model) for value in (own, other))

    def kernel(place_ref, own_ref, other_ref, result, *held):
        x, y, z, core = (place_ref[i] for i in range(4))
        target = held[0] if flip else result
        for side, ref in enumerate((own_ref, other_ref)):
            for step in range(RING):
                at_x = lax.rem(z + step - x + RING, RING)
                for low in range(2):
                    at_y = lax.rem(2 * lax.rem(core + side, 2) + low - y + RING, RING)
                    for owner in range(2):
                        second, first = (at_y, at_x) if owner == 0 else (at_x, at_y)
                        target[lax.rem(core + owner, 2), second, first] = ref[step, low, owner]
        if flip:
            for i in range(2 * RING):
                block = target[i // RING, i % RING].reshape(RING * half, model)
                result[:, i * RING * half : (i + 1) * RING * half] = block.T

    order = (2, RING, RING, half, model)
    shape = (model, 2 * RING * RING * half) if flip else order
    block = pl.BlockSpec((RING, 2, 2, half, model), lambda j: (0,) * 5)
    result = pl.pallas_call(
        kernel,
        grid=(1,),
        in_specs=[pl.BlockSpec(memory_space=pltpu.SMEM), block, block],
        out_specs=pl.BlockSpec(shape, lambda j: (0,) * len(shape)),
        out_shape=jax.ShapeDtypeStruct(shape, BF16),
        scratch_shapes=[pltpu.VMEM(order, BF16)] if flip else [],
        compiler_params=params(16),
        cost_estimate=light(),
        name="travel_order",
    )(place, own, other)
    return result if flip else result.reshape(2, RING, RING * half, model)


def down_products(tokens, groups):
    _, _, rows, model = tokens.shape
    parts = [part for group in groups for part in group]
    width = parts[0][1].shape[0]
    tile = 256
    operands, in_specs = [], []
    for k, weight, extras in parts:
        operands += [tokens, weight] + [stack for stack, _ in extras]
        in_specs.append(pl.BlockSpec((None, 1, rows, model), lambda j, k=k: (0, k, 0, 0)))
        in_specs.append(pl.BlockSpec((tile, model), lambda j: (j, 0)))
        for _, at in extras:
            in_specs.append(pl.BlockSpec((1, rows, tile), lambda j, at=at: (at, 0, j)))

    def kernel(*refs):
        at = 0
        for out, group in zip(refs[len(operands) :], groups):
            for n, (_, _, extras) in enumerate(group):
                total = lax.dot_general(
                    refs[at][0], refs[at + 1][...], LAST, preferred_element_type=F32
                )
                for i in range(len(extras)):
                    total = total + refs[at + 2 + i][0].astype(F32)
                at += 2 + len(extras)
                out[n] = total.astype(BF16)

    return pl.pallas_call(
        kernel,
        grid=(width // tile,),
        in_specs=in_specs,
        out_specs=[pl.BlockSpec((len(group), rows, tile), lambda j: (0, 0, j)) for group in groups],
        out_shape=[jax.ShapeDtypeStruct((len(group), rows, width), BF16) for group in groups],
        compiler_params=params(14),
        cost_estimate=light(),
        name="down_products",
    )(*operands)


def scatter_sum(tokens, weight, weight_other, before, between):
    (fwd,) = down_products(tokens, [[(2, weight, ()), (1, weight_other, ())]])
    (back,) = down_products(tokens, [[(2, weight_other, ()), (3, weight, ())]])
    fwd, back, *_ = lax.optimization_barrier((fwd, back, *before))
    fwd, back = mix(fwd, 2, 1), mix(back, 2, -1)
    own, other = down_products(
        tokens, [[(1, weight, ((fwd, 0),))], [(3, weight_other, ((back, 0),))]]
    )
    moved = between(own, other)
    own, other = mix(own, 2, 1), mix(other, 2, -1)
    (sums,) = down_products(
        tokens,
        [
            [
                (0, weight, ((own, 0), (back, 1))),
                (0, weight_other, ((fwd, 1), (other, 0))),
            ]
        ],
    )
    sums = sums.reshape(2, RING, -1, sums.shape[-1])
    total = tie(sums[:, 0], *moved).astype(F32)
    for distance, step in ((2, 2), (1, 1), (3, -1)):
        total = total + mix(sums[:, distance], 1, step).astype(F32)
    return total, moved


def first_gather(block):
    _, n, half, width = block.shape
    across, after, before = mix(block, 1, 2), mix(block, 1, -1), mix(block, 1, 1)
    return tuple(
        jnp.stack([piece[i] for piece in (block, after, across, before)], 1).reshape(
            n, RING * half, width
        )
        for i in range(2)
    )


def weight_grads(left, mine, theirs, flip=False):
    stacked = not isinstance(theirs, list)
    n, (_, rows, width) = (1, theirs.shape) if stacked else (mine[0].shape[0], mine[0].shape)
    ready = left.ndim == 2
    model = left.shape[0] if ready else left.shape[-1]
    if stacked:
        places = [at for _, at in mine] + list(range(RING))
        pieces = [stack for stack, _ in mine] + [theirs] * RING
    else:
        places, pieces = [0] * (2 * RING), [*mine, *theirs]
    tile = 256

    def kernel(left_ref, *refs):
        held = left_ref
        if not ready:
            held = refs[-1]

            @pl.when(pl.program_id(0) == 0)
            def _():
                for i in range(2 * RING):
                    held[:, i * rows : (i + 1) * rows] = left_ref[i // RING, i % RING].T

        for i in range(n):
            right = jnp.concatenate([ref[i] for ref in refs[: len(pieces)]], 0)
            result = jnp.dot(held[...], right, preferred_element_type=F32)
            refs[len(pieces) + i][...] = result.T if flip else result

    if flip:
        shape, out_spec = (width, model), pl.BlockSpec((tile, model), lambda j: (j, 0))
    else:
        shape, out_spec = (model, width), pl.BlockSpec((model, tile), lambda j: (0, j))
    scratch = [] if ready else [pltpu.VMEM((model, rows * len(pieces)), BF16)]
    return pl.pallas_call(
        kernel,
        grid=(width // tile,),
        in_specs=[pl.BlockSpec(left.shape, lambda j: (0,) * left.ndim)]
        + [pl.BlockSpec((n, rows, tile), lambda j, at=at: (at, 0, j)) for at in places],
        out_specs=[out_spec] * n,
        out_shape=[jax.ShapeDtypeStruct(shape, F32)] * n,
        scratch_shapes=scratch,
        compiler_params=params(18 if n > 1 else 14),
        cost_estimate=light(),
        name="weight_grads",
    )(left, *pieces)


def input_products(groups, ready=(), place=None, whole=True):
    last = place is not None
    terms = [term for group in groups for term in group]
    _, rows, width = terms[0][0].shape
    model = terms[0][1][0][0].shape[-2]
    tile = 256 if len(terms) > 1 else width // 2
    steps = width // tile
    half = rows // RING
    pairs = {id(weights): weights for _, weights in terms}
    order = list(pairs)
    weights = [weight for key in order for weight in pairs[key]]
    inputs = ([place] if last else []) + [piece for piece, _ in terms]
    inputs += [weight for weight, _ in weights] + list(ready)
    count = RING if last else len(groups)

    def kernel(*refs):
        ins, refs = refs[: len(inputs)], refs[len(inputs) :]
        outs, scratch = refs[:count], refs[count:]
        place_ref, ins = (ins[0], ins[1:]) if last else (None, ins)
        weight_refs, ready_refs = ins[len(terms) :][: len(weights)], ins[len(terms) + len(weights) :]
        total = scratch[0]
        step = pl.program_id(0)
        at = 0
        for p, group in enumerate(groups):
            value = None
            for _, own_weights in group:
                pair = 2 * order.index(id(own_weights))
                for i in range(2):
                    term = lax.dot_general(
                        ins[at][i], weight_refs[pair + i][...], LAST, preferred_element_type=F32
                    )
                    value = term if value is None else value + term
                at += 1

            @pl.when(step == 0)
            def _():
                total[p] = value

            @pl.when((step > 0) & (step < steps - 1))
            def _():
                total[p] += value

            @pl.when(step == steps - 1)
            def _():
                result = total[p] + value
                if not last:
                    outs[p][...] = result.astype(outs[p].dtype)
                    return
                held = scratch[1]
                x, y, z, core = (place_ref[i] for i in range(4))
                held[2] = (result + ready_refs[0][...]).astype(BF16).reshape(RING, half, model)
                for k, ref in zip((0, 1, 3), ready_refs[1:]):
                    held[k] = ref[...].reshape(RING, half, model)
                for distance in range(RING):
                    at_x = lax.rem(z + distance - x + RING, RING)
                    for j in range(2):
                        for low in range(2):
                            at_y = lax.rem(2 * lax.rem(core + j, 2) + low - y + RING, RING)
                            second = jnp.where(core == 0, at_y, at_x)
                            first = jnp.where(core == 0, at_x, at_y)
                            outs[distance][j, low] = held[second, first]

    scratch = [pltpu.VMEM((len(groups), rows, model), F32)]
    block = pl.BlockSpec((rows, model), lambda j: (0, 0))
    if last:
        scratch.append(pltpu.VMEM((RING, RING, half, model), BF16))
        out_specs = [pl.BlockSpec((2, 2, half, model), lambda j: (0, 0, 0, 0))] * RING
        out_shape = [jax.ShapeDtypeStruct((2, 2, half, model), BF16)] * RING
    else:
        out_specs = [block] * count
        out_shape = [jax.ShapeDtypeStruct((rows, model), BF16 if whole else F32)] * count
    return pl.pallas_call(
        kernel,
        grid=(steps,),
        in_specs=([pl.BlockSpec(memory_space=pltpu.SMEM)] if last else [])
        + [pl.BlockSpec((2, rows, tile), lambda j: (0, 0, j))] * len(terms)
        + [
            pl.BlockSpec((model, tile), lambda j: (0, j))
            if at is None
            else pl.BlockSpec((None, model, tile), lambda j, at=at: (at, 0, j))
            for _, at in weights
        ]
        + [block] * len(ready),
        out_specs=out_specs,
        out_shape=out_shape,
        scratch_shapes=scratch,
        compiler_params=params(16),
        cost_estimate=light(),
        name="input_products",
    )(*inputs)


def on_device(layer_input, gate_pre, up_pre, grad_out, w_gate, w_up, w_down):
    x, y, z, core = (lax.axis_index(name) for name in ("x", "y", "z", "c"))
    place = jnp.stack([x, y, z, core]).astype(jnp.int32)
    rows, width = gate_pre.shape
    half, model = rows // 2, w_down.shape[1]

    def half_of_tokens(value, shape):
        halves = value.reshape(shape)
        return jnp.stack([pick(halves, core, 1), swap(pick(halves, 1 - core, 1))])

    pre = half_of_tokens(jnp.stack([gate_pre, up_pre]), (2, 2, half, width))
    gate_val, up_val = pre[:, 0].astype(F32), pre[:, 1].astype(F32)
    sigmoid_val = jax.nn.sigmoid(gate_val)
    hidden = (gate_val * sigmoid_val * up_val).astype(BF16)[:, None]
    def from_z(value):
        return jnp.stack([value, along_z(value, -1), along_z(value, 2), along_z(value, 1)])

    hid = jnp.concatenate(first_gather(hidden))
    w_down_other = swap(tie(w_down, hidden))
    hid, w_down_other = lax.optimization_barrier((hid, w_down_other))
    hid_after, hid_before = mix(hid, 2, -1), mix(hid, 2, 1)

    out_blocks = from_z(tie(grad_out, hidden))
    tokens = travel_order(place, out_blocks, swap(out_blocks))

    def hidden_across(*after):
        return mix(tie(hid_before[1], *after), 2, 1), mix(tie(hid_after[0], *after), 2, -1)

    grad_hidden, (hid_other_across, hid_own_across) = scatter_sum(
        tokens, w_down, w_down_other, (hid_after, hid_before), hidden_across
    )
    hid_theirs = jnp.stack([hid[1], hid_after[1], hid_other_across, hid_before[1]])
    hid_theirs = swap(tie(hid_theirs, grad_hidden))

    gate_val, up_val = pre[:, 0].astype(F32), pre[:, 1].astype(F32)
    sigmoid_val = jax.nn.sigmoid(gate_val)
    gate_grad = grad_hidden * up_val * sigmoid_val * (1.0 + gate_val * (1.0 - sigmoid_val))
    up_grad = grad_hidden * (gate_val * sigmoid_val)
    own, other = first_gather(jnp.stack([gate_grad, up_grad], 1).astype(BF16))

    w_other = swap(tie(jnp.stack([w_gate, w_up]), grad_hidden))
    own, other, w_other, hid_theirs = lax.optimization_barrier(
        (own, other, w_other, hid_theirs)
    )
    own_after, other_before = mix(own, 2, -1), mix(other, 2, 1)

    (grad_down,) = weight_grads(
        tokens,
        [(hid, 0), (hid_after, 0), (hid_own_across[None], 0), (hid_before, 0)],
        hid_theirs,
        flip=True,
    )
    input_blocks = from_z(tie(layer_input, own))
    own_later, other_later, input_blocks, grad_down = lax.optimization_barrier(
        (own, other, input_blocks, grad_down)
    )
    own_before, other_after = mix(own_later, 2, 1), mix(other_later, 2, -1)
    input_left = travel_order(place, input_blocks, swap(input_blocks), flip=True)
    other_across, own_across = mix(other_before, 2, 1), mix(own_after, 2, -1)

    here, there = ((w_gate, None), (w_up, None)), ((w_other, 0), (w_other, 1))
    ready = input_products(
        [
            [(own, here), (other, there)],
            [(own_after, here), (other_after, there)],
            [(own_before, here), (other_before, there)],
        ]
    )
    other_across, input_left, *ready, theirs_here, theirs_before = lax.optimization_barrier(
        (other_across, input_left, *ready, swap(other_later), swap(other_before))
    )
    theirs = [theirs_here, swap(other_after), swap(other_across), theirs_before]
    (first,) = input_products([[(other_across, there)]], whole=False)
    parts = input_products([[(own_across, here)]], [first, *ready], place)
    grad_gate, grad_up = weight_grads(
        input_left,
        [own, own_after, own_across, own_before],
        theirs,
    )
    received = [along_z(parts[k], step) for k, step in ((2, 2), (1, 1), (3, -1))]
    total = tie(parts[0], grad_gate, grad_up).astype(F32)
    for part in received:
        total = total + part.astype(F32)
    total = total.astype(BF16)
    keep, got = total[0], swap(total[1])
    grad_input = jnp.where(
        core == 0, jnp.stack([keep, got], 1), jnp.stack([got, keep], 1)
    ).reshape(4 * half, model)

    return grad_input, grad_gate, grad_up, grad_down


def solution(mesh):
    chips = Mesh(mesh.devices.reshape(RING, RING, RING, 2), ("x", "y", "z", "c"))
    row, col = ("x", "y"), ("z", "c")
    in_specs = (
        P(col, row),
        P(row, col),
        P(row, col),
        P(col, row),
        P(row, col),
        P(row, col),
        P(col, row),
    )
    out_specs = (P(col, row), P(row, col), P(row, col), P(col, row))
    return jax.shard_map(
        on_device, mesh=chips, in_specs=in_specs, out_specs=out_specs, check_vma=False
    )
```
